256 devices in a mesh: seq: 16 (over y, x), head: 16 (over z, core).
Axes of the slice: x: 4, y: 4, z: 8, core: 2. Of those that a mesh axis runs over, the one named last changes fastest.
Arguments:
- inputs: bfloat16 [81920, 8192], P(('seq', 'head')), may hold values from -0.15625 to 0.15625
- log_decay: float32 [81920, 128], P(('seq', 'head')), may hold values from -2 to 0, as said below
- write_vectors: bfloat16 [81920, 1024], P(('seq', 'head')), may hold values from -6 to 6
- read_vectors: bfloat16 [81920, 1024], P(('seq', 'head')), may hold values from -0.5 to 0.5
Outputs:
- mixed: bfloat16 [81920, 8192], P(('seq', 'head'))
The draws below stay inside these ranges and needn't reach their ends.
Inputs may be any that keep to these rules, and one draw needn't show every extreme that they name: `log_decay`: every entry is negative.
All inputs are finite; a program needn't handle non-finite values.
Results may differ from the reference program's by a relative error of at most 0.0056.
Values may be sent and summed in bfloat16 or wider, within the bound.
No kernel may reach another device: no remote copies, remote signals or barrier semaphores. Data moves between devices by JAX's collectives and lax.ppermute only.
A program may use at most 128 MiB of HBM per device.

```python
import math
import jax
import jax.numpy as jnp
from jax import lax

H = 128
P_SIZE = 64
N = 128
G = 8
SPAN = 256
TOKENS = 81920


def draw_log_decay(key, part):
    key = jax.random.fold_in(key, 11)
    keys = jax.random.split(key, 7)
    share = 0.5
    quick = jax.random.uniform(keys[0], (H,)) < share
    quick_rate = jnp.exp(jax.random.uniform(keys[1], (H,), jnp.float32, math.log(1.0 / 50.0), math.log(1.0 / 30.0)))
    slow_rate = jnp.exp(jax.random.uniform(keys[2], (H,), jnp.float32, math.log(0.5 / TOKENS), math.log(0.25 / SPAN)))
    decay_speed = jnp.where(quick, quick_rate, slow_rate)
    coarse_estimate = jnp.exp(jax.random.uniform(keys[3], (TOKENS, H), jnp.float32, math.log(0.5), math.log(2.0)))
    per_block_outputs = jnp.exp(jax.random.uniform(keys[4], (TOKENS // SPAN, H), jnp.float32, math.log(0.5), math.log(2.0)))
    per_block_outputs = jnp.repeat(per_block_outputs, SPAN, axis=0)
    places = jax.random.randint(keys[5], (3,), 0, TOKENS)
    layer_depth_list = jax.random.uniform(keys[6], (3, H), jnp.float32, 0.223, 0.431)
    positions = jnp.arange(TOKENS, dtype=jnp.int32)
    match_tally = (positions[:, None] == places[None, :]).astype(jnp.float32)
    span_segments = jnp.dot(match_tally, layer_depth_list)
    return -(decay_speed[None, :] * coarse_estimate * per_block_outputs + span_segments)


def block_levels(own_key, extent, cuts, low, top_value):
    level, own = 1.0, jax.random.fold_in(own_key, 6)
    for position, blocks in cuts:
        draws = jnp.exp(jax.random.uniform(jax.random.fold_in(own, position), (blocks,), jnp.float32, low / len(cuts), top_value / len(cuts)))
        level = level * jnp.repeat(draws, extent[position] // blocks).reshape([-1 if axis == position else 1 for axis in range(len(extent))])
    return level


def centred(rng, dims, deviation, limit, cuts=(), kind=jnp.bfloat16):
    factor_of = block_levels(rng, dims, cuts, -0.22, 0.18) if cuts else 1.0
    result = jax.random.normal(rng, dims, jnp.float32) * deviation * factor_of
    return jnp.minimum(jnp.maximum(result, -limit), limit).astype(kind)


def setup_inputs(seed: int = 0) -> dict:
    splits = jax.random.split(jax.random.key(seed), 5)
    return {
        "inputs": centred(splits[0], (TOKENS, H * P_SIZE), (TOKENS // 64) ** -0.5, 0.15625, ((0, 256),)),
        "log_decay": draw_log_decay(jax.random.fold_in(splits[4], 71), 0),
        "write_vectors": centred(splits[2], (TOKENS, G * N), 1.0, 6.0, ((0, 256),)),
        "read_vectors": centred(splits[3], (TOKENS, G * N), N ** -0.5, 0.5, ((0, 256),)),
    }


def reference(inputs, log_decay, write_vectors, read_vectors):
    total = inputs.shape[0]
    spans = total // SPAN
    spread_heads = H // G
    blocked_x = inputs.reshape(spans, SPAN, H, P_SIZE)
    blocked_b = write_vectors.reshape(spans, SPAN, G, N)
    blocked_c = read_vectors.reshape(spans, SPAN, G, N)
    blocked_a = log_decay.reshape(spans, SPAN, H)
    order = jnp.arange(SPAN, dtype=jnp.int32)
    lower = order[:, None] >= order[None, :]

    def advance(state, block):
        block_x, block_b, block_c, block_a = block
        cumulative = jnp.cumsum(block_a, axis=0)
        scores = jnp.einsum("ign,jgn->gij", block_c.astype(jnp.float32), block_b.astype(jnp.float32))
        scores = jnp.repeat(scores, spread_heads, axis=0)
        cum_heads = cumulative.T
        spread = jnp.where(lower[None], cum_heads[:, :, None] - cum_heads[:, None, :], -jnp.inf)
        weights = (scores * jnp.exp(spread)).astype(jnp.bfloat16)
        weights = lax.optimization_barrier(weights).astype(jnp.float32)
        diagonal = jnp.einsum("hij,jhp->ihp", weights, block_x.astype(jnp.float32))
        heads_b = jnp.repeat(block_b, spread_heads, axis=1).astype(jnp.float32)
        heads_c = jnp.repeat(block_c, spread_heads, axis=1).astype(jnp.float32)
        held = lax.optimization_barrier(state.astype(jnp.bfloat16)).astype(jnp.float32)
        read_projection = jnp.einsum("ihn,hnp->ihp", heads_c, held) * jnp.exp(cumulative)[:, :, None]
        output = (diagonal + read_projection).astype(jnp.bfloat16)
        fading = jnp.exp(cumulative[-1][None, :] - cumulative)
        scaled = (fading[:, :, None] * heads_b).astype(jnp.bfloat16)
        scaled = lax.optimization_barrier(scaled).astype(jnp.float32)
        contribution = jnp.einsum("jhn,jhp->hnp", scaled, block_x.astype(jnp.float32))
        new_state = jnp.exp(cumulative[-1])[:, None, None] * state + contribution
        return new_state, output

    initial = jnp.zeros((H, N, P_SIZE), jnp.float32)
    _, outputs = lax.scan(advance, initial, (blocked_x, blocked_b, blocked_c, blocked_a))
    return outputs.reshape(total, H * P_SIZE)
```

```python
import math

import jax
import jax.numpy as jnp
from jax import lax
from jax.experimental import pallas as pl
from jax.experimental.pallas import tpu as pltpu
from jax.sharding import Mesh, PartitionSpec as P

G = 8
LOG2E = math.log2(math.e)
VMEM_LIMIT = 16 * 1024 * 1024
EXTRA = 8
F32 = jnp.float32
BF16 = jnp.bfloat16


def split_two(a):
    high = a.astype(BF16)
    return high, (a - high.astype(F32)).astype(BF16)


def split_three(a):
    high = a.astype(BF16)
    rest = a - high.astype(F32)
    middle, low = split_two(rest)
    return high, middle, low


def head_columns(columns, channels, heads):
    row = lax.broadcasted_iota(jnp.int32, (heads, columns), 0)
    col = lax.broadcasted_iota(jnp.int32, (heads, columns), 1)
    shift = channels.bit_length() - 1
    pick = jnp.where(row == lax.shift_right_logical(col, shift), 1.0, 0.0).astype(BF16)
    return jnp.concatenate([pick, pick], axis=0)


def spread_heads(values, pick, base):
    values = pltpu.roll(values, values.shape[1] - base, axis=1)
    high, low = split_two(values)
    return jnp.dot(jnp.concatenate([high, low], axis=1), pick, preferred_element_type=F32)


def group_columns(ref, group, columns):
    return ref.at[:, pl.ds(pl.multiple_of(group * columns, columns), columns)]


def decay_rows(total, pick, base):
    heads = total.shape[1]
    total = pltpu.roll(jnp.broadcast_to(total, (EXTRA, heads)), heads - base, axis=1)
    high, middle, low = (part.astype(F32) for part in split_three(total))
    row = lax.broadcasted_iota(jnp.int32, (EXTRA, heads), 0)
    sides = []
    for start in (0, 3):
        rows = jnp.where(row == start, high, jnp.where(row == start + 1, middle, jnp.where(row == start + 2, low, 0.0)))
        sides.append(jnp.dot(rows.astype(BF16), pick[:heads], preferred_element_type=F32))
    return sides


def log_decays(rows):
    rows = rows.astype(F32)
    return tuple(rows[i + 2 : i + 3] + rows[i + 1 : i + 2] + rows[i : i + 1] for i in (0, 3))


def pack_decays(first, second):
    parts = [part.astype(F32) for whole in (first, second) for part in split_three(whole)]
    parts.append(jnp.zeros((EXTRA - len(parts), first.shape[1]), F32))
    return jnp.concatenate(parts, axis=0).astype(BF16)


def running_sum(a):
    length = a.shape[0]
    row = lax.broadcasted_iota(jnp.int32, (length, length), 0)
    col = lax.broadcasted_iota(jnp.int32, (length, length), 1)
    lower = jnp.where(row >= col, 1.0, 0.0).astype(BF16)
    high, middle, low = split_three(a)
    return (
        jnp.dot(lower, low, preferred_element_type=F32)
        + jnp.dot(lower, middle, preferred_element_type=F32)
        + jnp.dot(lower, high, preferred_element_type=F32)
    )


def write_group(channels, group, turn, x, writers, fade, total, pick, state_ref):
    columns = x.shape[1]
    base = group * (columns // channels)
    high, low = split_two(x.astype(F32) * spread_heads(fade, pick, base))
    state = lax.dot_general(
        jnp.concatenate([writers, writers], axis=0),
        jnp.concatenate([high, low], axis=0),
        (((0,), (0,)), ((), ())),
        preferred_element_type=F32,
    ).astype(BF16)
    decays = decay_rows(total, pick, base)
    blocks_n, blocks_c, rows, lanes = state_ref.shape
    rows = (rows - EXTRA) // 2
    count = columns // lanes // 2
    for j in range(count):
        left, middle, right = (k * lanes for k in (2 * j, 2 * j + 1, 2 * j + 2))
        extra = (decays[0][:, left:middle] + decays[1][:, middle:right]).astype(BF16)
        for i in range(blocks_n):
            span = slice(i * rows, (i + 1) * rows)
            state_ref[i, turn * count + j, :rows] = state[span, left:middle]
            state_ref[i, turn * count + j, rows : 2 * rows] = state[span, middle:right]
            state_ref[i, turn * count + j, 2 * rows :] = extra


def first_kernel(channels, side_ref, a_hbm, x_hbm, b_hbm, cum_ref, state_ref, x_ref, b_ref, fade_ref, pick_ref, a_sem, x_sems, b_sems):
    columns = x_ref.shape[1] // G
    state_size = b_ref.shape[1] // G
    half = G // 2
    length, heads = cum_ref.shape
    bring = pltpu.make_async_copy(a_hbm, cum_ref, a_sem)
    bring.start()
    copies = []
    for turn in range(G):
        side = side_ref[0] if turn < half else 1 - side_ref[0]
        group = side * half + turn % half
        pair = (
            pltpu.make_async_copy(
                group_columns(b_hbm, group, state_size), group_columns(b_ref, group, state_size), b_sems.at[turn]
            ),
            pltpu.make_async_copy(
                group_columns(x_hbm, group, columns), group_columns(x_ref, group, columns), x_sems.at[turn]
            ),
        )
        for copy in pair:
            copy.start()
        copies.append((group, pair))
    pick = head_columns(columns, channels, heads)
    bring.wait()
    cum = running_sum(cum_ref[...])
    cum_ref[...] = cum
    total = cum[length - 1 :, :]
    fade_ref[...] = jnp.exp(jnp.minimum(total - cum, 0.0))
    pick_ref[...] = pick
    for turn, (group, pair) in enumerate(copies):
        for copy in pair:
            copy.wait()
        if turn < half:
            write_group(
                channels, group, turn,
                group_columns(x_ref, group, columns)[...],
                group_columns(b_ref, group, state_size)[...],
                fade_ref[...], total, pick_ref[...], state_ref,
            )


def second_kernel(channels, side_ref, cum_ref, x_ref, b_ref, state_ref, fade_ref, pick_ref):
    columns = x_ref.shape[1] // G
    state_size = b_ref.shape[1] // G
    half = G // 2
    length, heads = cum_ref.shape
    cum = cum_ref[...]
    total = cum[length - 1 :, :]
    fade_ref[...] = jnp.exp(jnp.minimum(total - cum, 0.0))
    pick_ref[...] = head_columns(columns, channels, heads)
    for turn in range(half):
        group = side_ref[0] * half + turn
        write_group(
            channels, group, turn,
            group_columns(x_ref, group, columns)[...],
            group_columns(b_ref, group, state_size)[...],
            fade_ref[...], total, pick_ref[...], state_ref,
        )


WHOLE = pl.BlockSpec(memory_space=pltpu.VMEM)
SCALAR = pl.BlockSpec(memory_space=pltpu.SMEM)
LEFT = pl.BlockSpec(memory_space=pltpu.HBM)


def state_shape(length, width, state_size, pieces_n, pieces_c):
    lanes = width // 2 // pieces_c // 2
    return jax.ShapeDtypeStruct((pieces_n, pieces_c, 2 * state_size // pieces_n + EXTRA, lanes), BF16)


def first_states(side, log_decay, inputs, write_vectors, pieces_n, pieces_c):
    length, heads = log_decay.shape
    width = inputs.shape[1]
    return pl.pallas_call(
        lambda *refs: first_kernel(width // heads, *refs),
        in_specs=[SCALAR, LEFT, LEFT, LEFT],
        out_specs=[WHOLE] * 4,
        out_shape=[
            jax.ShapeDtypeStruct(log_decay.shape, F32),
            state_shape(length, width, write_vectors.shape[1] // G, pieces_n, pieces_c),
            jax.ShapeDtypeStruct(inputs.shape, BF16),
            jax.ShapeDtypeStruct(write_vectors.shape, BF16),
        ],
        scratch_shapes=[
            pltpu.VMEM((length, heads), F32),
            pltpu.VMEM((2 * heads, width // G), BF16),
            pltpu.SemaphoreType.DMA,
            pltpu.SemaphoreType.DMA((G,)),
            pltpu.SemaphoreType.DMA((G,)),
        ],
        compiler_params=pltpu.CompilerParams(vmem_limit_bytes=VMEM_LIMIT),
        cost_estimate=pl.CostEstimate(flops=2 * length * 256 * width, bytes_accessed=4 * inputs.size, transcendentals=0),
    )(side, *(pltpu.with_memory_space_constraint(a, pltpu.HBM) for a in (log_decay, inputs, write_vectors)))


def second_states(side, cumulative, inputs, write_vectors, pieces_n, pieces_c):
    length, heads = cumulative.shape
    width = inputs.shape[1]
    return pl.pallas_call(
        lambda *refs: second_kernel(width // heads, *refs),
        in_specs=[SCALAR, WHOLE, WHOLE, WHOLE],
        out_specs=WHOLE,
        out_shape=state_shape(length, width, write_vectors.shape[1] // G, pieces_n, pieces_c),
        scratch_shapes=[pltpu.VMEM((length, heads), F32), pltpu.VMEM((2 * heads, width // G), BF16)],
        compiler_params=pltpu.CompilerParams(vmem_limit_bytes=VMEM_LIMIT),
        cost_estimate=pl.CostEstimate(flops=2 * length * 256 * width, bytes_accessed=inputs.size, transcendentals=0),
    )(side, cumulative, inputs, write_vectors)


def join_kernel(side_ref, kept_ref, came_ref, out_ref):
    blocks_n, blocks_c, rows, _ = kept_ref.shape
    rows = (rows - EXTRA) // 2

    def join(first_ref, second_ref):
        for j in range(blocks_c):
            before = log_decays(first_ref[0, j, 2 * rows :])
            after = log_decays(second_ref[0, j, 2 * rows :])
            extra = pack_decays(*(a + b for a, b in zip(before, after)))
            for k in range(2):
                span = slice(k * rows, (k + 1) * rows)
                decay = jnp.exp(after[k])
                for i in range(blocks_n):
                    out_ref[i, j, span] = (
                        decay * first_ref[i, j, span].astype(F32) + second_ref[i, j, span].astype(F32)
                    ).astype(BF16)
            for i in range(blocks_n):
                out_ref[i, j, 2 * rows :] = extra

    @pl.when(side_ref[0] == 0)
    def _():
        join(kept_ref, came_ref)

    @pl.when(side_ref[0] == 1)
    def _():
        join(came_ref, kept_ref)


def on_chip(kernel, shape, side, *arrays):
    whole = pl.BlockSpec(memory_space=pltpu.VMEM)
    return pl.pallas_call(
        kernel,
        in_specs=[pl.BlockSpec(memory_space=pltpu.SMEM)] + [whole] * len(arrays),
        out_specs=whole,
        out_shape=jax.ShapeDtypeStruct(shape, BF16),
        compiler_params=pltpu.CompilerParams(vmem_limit_bytes=VMEM_LIMIT),
    )(side, *arrays)


def joined(side, kept, came):
    return on_chip(join_kernel, kept.shape, side, kept, came)


def give_kernel(side_ref, held_ref, kept_ref, out_ref):
    blocks_n, blocks_c, rows, _ = held_ref.shape
    rows = rows // 2

    @pl.when(side_ref[0] == 0)
    def _():
        for j in range(blocks_c):
            logs = log_decays(kept_ref[0, j, 2 * rows :])
            for k in range(2):
                span = slice(k * rows, (k + 1) * rows)
                decay = jnp.exp(logs[k])
                for i in range(blocks_n):
                    out_ref[i, j, span] = (
                        decay * held_ref[i, j, span].astype(F32) + kept_ref[i, j, span].astype(F32)
                    ).astype(BF16)

    @pl.when(side_ref[0] == 1)
    def _():
        out_ref[...] = held_ref[...]


def given(side, held, kept):
    return on_chip(give_kernel, held.shape, side, held, kept)


def diagonal_kernel(channels, side_ref, cum_ref, x_ref, b_ref, c_ref, out_ref, cum_rows, cum_cols, scores):
    length, heads = cum_ref.shape
    columns = x_ref.shape[1] // G
    state_size = b_ref.shape[1] // G
    per_group = columns // channels
    half = G // 2
    padded = cum_rows.shape[1]

    scaled = cum_ref[...] * LOG2E
    cum_cols[...] = scaled
    tall = jnp.concatenate([scaled, jnp.zeros((padded - length, heads), F32)], axis=0)
    cum_rows[...] = tall.T

    def one(turn, _):
        group = turn + side_ref[0] * half
        diagonal_group(
            channels, group, cum_rows, cum_cols, scores,
            group_columns(x_ref, group, columns),
            group_columns(b_ref, group, state_size)[...],
            group_columns(c_ref, group, state_size)[...],
            group_columns(out_ref, turn, columns),
        )
        return 0

    lax.fori_loop(0, half, one, 0)


def diagonal_group(channels, group, cum_rows, cum_cols, scores, x_ref, writers, readers, out_ref):
    length, heads = cum_cols.shape
    per_group = x_ref.shape[1] // channels
    tile = 128
    sc = lax.dot_general(
        readers, writers, (((1,), (1,)), ((), ())), preferred_element_type=F32
    )
    row = lax.broadcasted_iota(jnp.int32, (length, length), 0)
    col = lax.broadcasted_iota(jnp.int32, (length, length), 1)
    scores[...] = jnp.where(row >= col, sc, 0.0)

    base = pl.multiple_of(group * per_group, per_group)
    rows_all = cum_rows[pl.ds(base, per_group), :]
    cols_all = pltpu.roll(cum_cols[...], heads - base, axis=1)
    starts = list(range(0, length, tile))

    def weights(head, top, bottom):
        column = cols_all[top:bottom, head : head + 1]
        parts = []
        for left in range(0, bottom, tile):
            right = min(left + tile, bottom)
            gap = column - rows_all[head : head + 1, left:right]
            if right > top:
                gap = jnp.minimum(gap, 0.0)
            parts.append((jnp.exp2(gap) * scores[top:bottom, left:right]).astype(BF16))
        return parts[0] if len(parts) == 1 else jnp.concatenate(parts, axis=1)

    lane = lax.broadcasted_iota(jnp.int32, (1, 2 * channels), 1)
    for pair in range(per_group // 2):
        x_pair = x_ref[:, pair * 2 * channels : (pair + 1) * 2 * channels]
        for top in starts:
            bottom = min(top + tile, length)
            both = jnp.concatenate(
                [weights(2 * pair, top, bottom), weights(2 * pair + 1, top, bottom)], axis=0
            )
            mixed = jnp.dot(both, x_pair[:bottom], preferred_element_type=F32)
            out_ref[top:bottom, pair * 2 * channels : (pair + 1) * 2 * channels] = jnp.where(
                lane < channels, mixed[: bottom - top], mixed[bottom - top :]
            )


def diagonals(side, cumulative, inputs, write_vectors, read_vectors):
    length, heads = cumulative.shape
    width = inputs.shape[1]
    padded = -(-length // 128) * 128
    return pl.pallas_call(
        lambda *refs: diagonal_kernel(width // heads, *refs),
        in_specs=[SCALAR] + [WHOLE] * 4,
        out_specs=WHOLE,
        out_shape=jax.ShapeDtypeStruct((length, width // 2), F32),
        scratch_shapes=[
            pltpu.VMEM((heads, padded), F32),
            pltpu.VMEM((length, heads), F32),
            pltpu.VMEM((length, length), F32),
        ],
        compiler_params=pltpu.CompilerParams(vmem_limit_bytes=VMEM_LIMIT),
        cost_estimate=pl.CostEstimate(
            flops=length * length * width,
            bytes_accessed=3 * length * width,
            transcendentals=length * length * heads // 2,
        ),
    )(side, cumulative, inputs, write_vectors, read_vectors)


def scan_kernel(side_ref, term_ref, out_ref):
    chips, rows, lanes = out_ref.shape
    rows = rows // 2
    block = 8

    def some(i, states):
        for k in range(block):
            at = i * block + k
            decays = log_decays(term_ref[at, 2 * rows :])
            after = []
            for side in range(2):
                span = slice(side * rows, (side + 1) * rows)
                out_ref[at, span] = states[side].astype(BF16)
                after.append(jnp.exp(decays[side]) * states[side] + term_ref[at, span].astype(F32))
            states = tuple(after)
        return states

    lax.fori_loop(0, chips // block, some, (jnp.zeros((rows, lanes), F32),) * 2)


def entries(side, terms):
    chips, rows, lanes = terms.shape
    return on_chip(scan_kernel, (chips, rows - EXTRA, lanes), side, terms)


def read_kernel(channels, mine, side_ref, cum_ref, c_ref, diagonal_ref, held_ref, *rest):
    out_hbm, grown_ref, pick_ref, out_ref, sems = rest[-5:]
    half, _, columns = out_ref.shape
    state_size = c_ref.shape[1] // G
    grown_ref[...] = jnp.exp(cum_ref[...])
    pick_ref[...] = head_columns(columns, channels, cum_ref.shape[1])
    blocks_n, blocks_c, rows, lanes = held_ref.shape
    rows = rows // 2
    count = blocks_c // half
    copies = []
    for turn in range(half):
        group = side_ref[0] * half + turn
        decay = spread_heads(grown_ref[...], pick_ref[...], group * (columns // channels))
        readers = group_columns(c_ref, group, state_size)[...]
        if mine:
            readers = jnp.concatenate([readers, readers], axis=1)
        for j in range(count):
            sides = []
            for k in range(2):
                at = turn * count + j
                span = slice(k * rows, (k + 1) * rows)
                held = jnp.concatenate([held_ref[i, at, span] for i in range(blocks_n)], axis=0)
                if mine:
                    came_ref = rest[0]
                    second = side_ref[0] == 1
                    came = jnp.concatenate([came_ref[i, at, span] for i in range(blocks_n)], axis=0)
                    logs = log_decays(came_ref[0, at, 2 * rows :])[k]
                    scale = jnp.exp(jnp.where(second, logs, 0.0))
                    start = scale * held.astype(F32) + jnp.where(second, came.astype(F32), 0.0)
                    held = jnp.concatenate(split_two(start), axis=0)
                sides.append(held)
            read = jnp.dot(readers, jnp.concatenate(sides, axis=1), preferred_element_type=F32)
            span = slice(2 * j * lanes, (2 * j + 2) * lanes)
            wide = slice(turn * columns + 2 * j * lanes, turn * columns + (2 * j + 2) * lanes)
            out_ref[turn, :, span] = (diagonal_ref[:, wide] + read * decay[:, span]).astype(BF16)
        copy = pltpu.make_async_copy(out_ref.at[turn], group_columns(out_hbm, group, columns), sems.at[turn])
        copy.start()
        copies.append(copy)
    for copy in copies:
        copy.wait()


def outputs(side, cumulative, read_vectors, diagonal, held, came=None, done=None):
    length, heads = cumulative.shape
    half = G // 2
    width = diagonal.shape[1] * 2
    columns = width // G
    in_specs = [SCALAR] + [WHOLE] * 4
    args = [side, cumulative, read_vectors, diagonal, held]
    aliases = {}
    if came is not None:
        in_specs.append(WHOLE)
        args.append(came)
    if done is not None:
        in_specs.append(LEFT)
        aliases = {len(args): 0}
        args.append(done)
    return pl.pallas_call(
        lambda *refs: read_kernel(width // heads, came is not None, *refs),
        in_specs=in_specs,
        out_specs=LEFT,
        scratch_shapes=[
            pltpu.VMEM((length, heads), F32),
            pltpu.VMEM((2 * heads, columns), BF16),
            pltpu.VMEM((half, length, columns), BF16),
            pltpu.SemaphoreType.DMA((half,)),
        ],
        out_shape=jax.ShapeDtypeStruct((length, width), BF16),
        input_output_aliases=aliases,
        compiler_params=pltpu.CompilerParams(vmem_limit_bytes=VMEM_LIMIT),
        cost_estimate=pl.CostEstimate(
            flops=2 * length * 128 * width,
            bytes_accessed=2 * length * width,
            transcendentals=0,
        ),
    )(*args)


def shards(inputs, log_decay, write_vectors, read_vectors):
    chips = lax.axis_size("seq") * lax.axis_size("z")
    pieces_n = 8
    pieces_c = chips // pieces_n
    own_side = lax.axis_index("c").astype(jnp.int32).reshape(1)
    other_side = 1 - own_side
    swap = [(0, 1), (1, 0)]

    cumulative, gone, inputs, write_vectors = first_states(
        other_side, log_decay, inputs, write_vectors, pieces_n, pieces_c
    )
    came = lax.ppermute(gone, "c", swap)
    kept = second_states(own_side, cumulative, inputs, write_vectors, pieces_n, pieces_c)
    term = joined(own_side, kept, came)

    terms = lax.all_to_all(term.reshape((chips,) + term.shape[2:]), ("seq", "z"), 0, 0, tiled=True)
    diagonal_own = diagonals(own_side, cumulative, inputs, write_vectors, read_vectors)
    terms, diagonal_own = lax.optimization_barrier((terms, diagonal_own))

    held = lax.all_to_all(entries(own_side, terms), ("seq", "z"), 0, 0, tiled=True)
    diagonal_other = diagonals(other_side, cumulative, inputs, write_vectors, read_vectors)
    held, diagonal_other = lax.optimization_barrier((held, diagonal_other))
    held = held.reshape(term.shape[:2] + held.shape[1:])

    held_other = lax.ppermute(given(own_side, held, kept), "c", swap)
    done = outputs(own_side, cumulative, read_vectors, diagonal_own, held, came=came)
    return outputs(other_side, cumulative, read_vectors, diagonal_other, held_other, done=done)


def solution(mesh):
    seq, head = mesh.devices.shape
    fine = Mesh(mesh.devices.reshape(seq, head // 2, 2), ("seq", "z", "c"))
    spec = P(("seq", "z", "c"), None)
    return jax.shard_map(
        shards, mesh=fine, in_specs=(spec,) * 4, out_specs=spec, check_vma=False
    )
```

```python
import functools
import math

import jax
import jax.numpy as jnp
from jax import lax
from jax.experimental import pallas as pl
from jax.experimental.pallas import tpu as pltpu
from jax.sharding import Mesh, PartitionSpec as P

G = 8
LOG2E = math.log2(math.e)
VMEM_LIMIT = 16 * 1024 * 1024
EXTRA = 8
F32 = jnp.float32
BF16 = jnp.bfloat16


def split_two(a):
    high = a.astype(BF16)
    return high, (a - high.astype(F32)).astype(BF16)


def split_three(a):
    high = a.astype(BF16)
    rest = a - high.astype(F32)
    middle, low = split_two(rest)
    return high, middle, low


def head_columns(columns, channels, heads):
    row = lax.broadcasted_iota(jnp.int32, (heads, columns), 0)
    col = lax.broadcasted_iota(jnp.int32, (heads, columns), 1)
    shift = channels.bit_length() - 1
    pick = jnp.where(row == lax.shift_right_logical(col, shift), 1.0, 0.0).astype(BF16)
    return jnp.concatenate([pick, pick], axis=0)


def spread_heads(values, pick, base):
    values = pltpu.roll(values, values.shape[1] - base, axis=1)
    high, low = split_two(values)
    return jnp.dot(jnp.concatenate([high, low], axis=1), pick, preferred_element_type=F32)


def group_columns(ref, group, columns):
    return ref.at[:, pl.ds(pl.multiple_of(group * columns, columns), columns)]


def decay_rows(total, pick, base):
    heads = total.shape[1]
    total = pltpu.roll(jnp.broadcast_to(total, (EXTRA, heads)), heads - base, axis=1)
    high, middle, low = (part.astype(F32) for part in split_three(total))
    row = lax.broadcasted_iota(jnp.int32, (EXTRA, heads), 0)
    sides = []
    for start in (0, 3):
        rows = jnp.where(row == start, high, jnp.where(row == start + 1, middle, jnp.where(row == start + 2, low, 0.0)))
        sides.append(jnp.dot(rows.astype(BF16), pick[:heads], preferred_element_type=F32))
    return sides


def log_decays(rows):
    rows = rows.astype(F32)
    return tuple(rows[i + 2 : i + 3] + rows[i + 1 : i + 2] + rows[i : i + 1] for i in (0, 3))


def pack_decays(first, second):
    parts = [part.astype(F32) for whole in (first, second) for part in split_three(whole)]
    parts.append(jnp.zeros((EXTRA - len(parts), first.shape[1]), F32))
    return jnp.concatenate(parts, axis=0).astype(BF16)


def running_sum(a):
    length = a.shape[0]
    row = lax.broadcasted_iota(jnp.int32, (length, length), 0)
    col = lax.broadcasted_iota(jnp.int32, (length, length), 1)
    lower = jnp.where(row >= col, 1.0, 0.0).astype(BF16)
    high, middle, low = split_three(a)
    return (
        jnp.dot(lower, low, preferred_element_type=F32)
        + jnp.dot(lower, middle, preferred_element_type=F32)
        + jnp.dot(lower, high, preferred_element_type=F32)
    )


def write_group(channels, group, turn, x, writers, fade, total, pick, state_ref):
    columns = x.shape[1]
    base = group * (columns // channels)
    high, low = split_two(x.astype(F32) * spread_heads(fade, pick, base))
    state = lax.dot_general(
        jnp.concatenate([writers, writers], axis=0),
        jnp.concatenate([high, low], axis=0),
        (((0,), (0,)), ((), ())),
        preferred_element_type=F32,
    ).astype(BF16)
    decays = decay_rows(total, pick, base)
    blocks_n, blocks_c, rows, lanes = state_ref.shape
    rows = (rows - EXTRA) // 2
    count = columns // lanes // 2
    for j in range(count):
        left, middle, right = (k * lanes for k in (2 * j, 2 * j + 1, 2 * j + 2))
        extra = (decays[0][:, left:middle] + decays[1][:, middle:right]).astype(BF16)
        for i in range(blocks_n):
            span = slice(i * rows, (i + 1) * rows)
            state_ref[i, turn * count + j, :rows] = state[span, left:middle]
            state_ref[i, turn * count + j, rows : 2 * rows] = state[span, middle:right]
            state_ref[i, turn * count + j, 2 * rows :] = extra


def first_kernel(channels, side_ref, a_hbm, x_hbm, b_hbm, cum_ref, state_ref, x_ref, b_ref, fade_ref, pick_ref, a_sem, x_sems, b_sems):
    columns = x_ref.shape[1] // G
    state_size = b_ref.shape[1] // G
    half = G // 2
    length, heads = cum_ref.shape
    bring = pltpu.make_async_copy(a_hbm, cum_ref, a_sem)
    bring.start()
    copies = []
    for turn in range(G):
        side = side_ref[0] if turn < half else 1 - side_ref[0]
        group = side * half + turn % half
        pair = (
            pltpu.make_async_copy(
                group_columns(b_hbm, group, state_size), group_columns(b_ref, group, state_size), b_sems.at[turn]
            ),
            pltpu.make_async_copy(
                group_columns(x_hbm, group, columns), group_columns(x_ref, group, columns), x_sems.at[turn]
            ),
        )
        for copy in pair:
            copy.start()
        copies.append((group, pair))
    pick = head_columns(columns, channels, heads)
    bring.wait()
    cum = running_sum(cum_ref[...])
    cum_ref[...] = cum
    total = cum[length - 1 :, :]
    fade_ref[...] = jnp.exp(jnp.minimum(total - cum, 0.0))
    pick_ref[...] = pick
    for turn, (group, pair) in enumerate(copies):
        for copy in pair:
            copy.wait()
        if turn < half:
            write_group(
                channels, group, turn,
                group_columns(x_ref, group, columns)[...],
                group_columns(b_ref, group, state_size)[...],
                fade_ref[...], total, pick_ref[...], state_ref,
            )


def second_kernel(channels, side_ref, cum_ref, x_ref, b_ref, state_ref, fade_ref, pick_ref):
    columns = x_ref.shape[1] // G
    state_size = b_ref.shape[1] // G
    half = G // 2
    length, heads = cum_ref.shape
    cum = cum_ref[...]
    total = cum[length - 1 :, :]
    fade_ref[...] = jnp.exp(jnp.minimum(total - cum, 0.0))
    pick_ref[...] = head_columns(columns, channels, heads)
    for turn in range(half):
        group = side_ref[0] * half + turn
        write_group(
            channels, group, turn,
            group_columns(x_ref, group, columns)[...],
            group_columns(b_ref, group, state_size)[...],
            fade_ref[...], total, pick_ref[...], state_ref,
        )


WHOLE = pl.BlockSpec(memory_space=pltpu.VMEM)
SCALAR = pl.BlockSpec(memory_space=pltpu.SMEM)
LEFT = pl.BlockSpec(memory_space=pltpu.HBM)


def state_shape(length, width, state_size, pieces_n, pieces_c):
    lanes = width // 2 // pieces_c // 2
    return jax.ShapeDtypeStruct((pieces_n, pieces_c, 2 * state_size // pieces_n + EXTRA, lanes), BF16)


def first_states(side, log_decay, inputs, write_vectors, pieces_n, pieces_c):
    length, heads = log_decay.shape
    width = inputs.shape[1]
    return pl.pallas_call(
        lambda *refs: first_kernel(width // heads, *refs),
        in_specs=[SCALAR, LEFT, LEFT, LEFT],
        out_specs=[WHOLE] * 4,
        out_shape=[
            jax.ShapeDtypeStruct(log_decay.shape, F32),
            state_shape(length, width, write_vectors.shape[1] // G, pieces_n, pieces_c),
            jax.ShapeDtypeStruct(inputs.shape, BF16),
            jax.ShapeDtypeStruct(write_vectors.shape, BF16),
        ],
        scratch_shapes=[
            pltpu.VMEM((length, heads), F32),
            pltpu.VMEM((2 * heads, width // G), BF16),
            pltpu.SemaphoreType.DMA,
            pltpu.SemaphoreType.DMA((G,)),
            pltpu.SemaphoreType.DMA((G,)),
        ],
        compiler_params=pltpu.CompilerParams(vmem_limit_bytes=VMEM_LIMIT),
        cost_estimate=pl.CostEstimate(flops=2 * length * 256 * width, bytes_accessed=4 * inputs.size, transcendentals=0),
    )(side, *(pltpu.with_memory_space_constraint(a, pltpu.HBM) for a in (log_decay, inputs, write_vectors)))


def second_states(side, cumulative, inputs, write_vectors, pieces_n, pieces_c):
    length, heads = cumulative.shape
    width = inputs.shape[1]
    return pl.pallas_call(
        lambda *refs: second_kernel(width // heads, *refs),
        in_specs=[SCALAR, WHOLE, WHOLE, WHOLE],
        out_specs=WHOLE,
        out_shape=state_shape(length, width, write_vectors.shape[1] // G, pieces_n, pieces_c),
        scratch_shapes=[pltpu.VMEM((length, heads), F32), pltpu.VMEM((2 * heads, width // G), BF16)],
        compiler_params=pltpu.CompilerParams(vmem_limit_bytes=VMEM_LIMIT),
        cost_estimate=pl.CostEstimate(flops=2 * length * 256 * width, bytes_accessed=inputs.size, transcendentals=0),
    )(side, cumulative, inputs, write_vectors)


def join_kernel(parts, side_ref, kept_ref, came_ref, out_hbm, out_ref, sems):
    blocks_n, blocks_c, rows, _ = kept_ref.shape
    rows = (rows - EXTRA) // 2

    def join(first_ref, second_ref):
        for j in range(blocks_c):
            before = log_decays(first_ref[0, j, 2 * rows :])
            after = log_decays(second_ref[0, j, 2 * rows :])
            extra = pack_decays(*(a + b for a, b in zip(before, after)))
            for k in range(2):
                span = slice(k * rows, (k + 1) * rows)
                decay = jnp.exp(after[k])
                for i in range(blocks_n):
                    out_ref[i, j, span] = (
                        decay * first_ref[i, j, span].astype(F32) + second_ref[i, j, span].astype(F32)
                    ).astype(BF16)
            for i in range(blocks_n):
                out_ref[i, j, 2 * rows :] = extra
            if (j + 1) % (blocks_c // parts) == 0:
                part_copy(parts, j * parts // blocks_c, out_ref, out_hbm, sems).start()

    @pl.when(side_ref[0] == 0)
    def _():
        join(kept_ref, came_ref)

    @pl.when(side_ref[0] == 1)
    def _():
        join(came_ref, kept_ref)

    for part in range(parts):
        part_copy(parts, part, out_ref, out_hbm, sems).wait()


def on_chip(kernel, shape, side, *arrays):
    whole = pl.BlockSpec(memory_space=pltpu.VMEM)
    return pl.pallas_call(
        kernel,
        in_specs=[pl.BlockSpec(memory_space=pltpu.SMEM)] + [whole] * len(arrays),
        out_specs=whole,
        out_shape=jax.ShapeDtypeStruct(shape, BF16),
        compiler_params=pltpu.CompilerParams(vmem_limit_bytes=VMEM_LIMIT),
    )(side, *arrays)


def off_chip(kernel, shape, side, *arrays):
    parts = 4
    whole = pl.BlockSpec(memory_space=pltpu.VMEM)
    return pl.pallas_call(
        functools.partial(kernel, parts),
        in_specs=[pl.BlockSpec(memory_space=pltpu.SMEM)] + [whole] * len(arrays),
        out_specs=LEFT,
        out_shape=pltpu.HBM(shape, BF16),
        scratch_shapes=[pltpu.VMEM(shape, BF16), pltpu.SemaphoreType.DMA((parts,))],
        compiler_params=pltpu.CompilerParams(vmem_limit_bytes=VMEM_LIMIT),
    )(side, *arrays)


def part_copy(parts, part, out_ref, out_hbm, sems):
    size = out_ref.shape[1] // parts
    span = pl.ds(part * size, size)
    return pltpu.make_async_copy(out_ref.at[:, span], out_hbm.at[:, span], sems.at[part])


def joined(side, kept, came):
    return off_chip(join_kernel, kept.shape, side, kept, came)


def give_kernel(side_ref, held_ref, kept_ref, out_ref):
    blocks_n, blocks_c, rows, _ = held_ref.shape
    rows = rows // 2

    @pl.when(side_ref[0] == 0)
    def _():
        for j in range(blocks_c):
            logs = log_decays(kept_ref[0, j, 2 * rows :])
            for k in range(2):
                span = slice(k * rows, (k + 1) * rows)
                decay = jnp.exp(logs[k])
                for i in range(blocks_n):
                    out_ref[i, j, span] = (
                        decay * held_ref[i, j, span].astype(F32) + kept_ref[i, j, span].astype(F32)
                    ).astype(BF16)

    @pl.when(side_ref[0] == 1)
    def _():
        out_ref[...] = held_ref[...]


def given(side, held, kept):
    return on_chip(give_kernel, held.shape, side, held, kept)


def diagonal_kernel(channels, side_ref, cum_ref, x_ref, b_ref, c_ref, out_ref, cum_rows, cum_cols, scores):
    length, heads = cum_ref.shape
    columns = x_ref.shape[1] // G
    state_size = b_ref.shape[1] // G
    per_group = columns // channels
    half = G // 2
    padded = cum_rows.shape[1]

    scaled = cum_ref[...] * LOG2E
    cum_cols[...] = scaled
    tall = jnp.concatenate([scaled, jnp.zeros((padded - length, heads), F32)], axis=0)
    cum_rows[...] = tall.T

    def one(turn, _):
        group = turn + side_ref[0] * half
        diagonal_group(
            channels, group, cum_rows, cum_cols, scores,
            group_columns(x_ref, group, columns),
            group_columns(b_ref, group, state_size)[...],
            group_columns(c_ref, group, state_size)[...],
            group_columns(out_ref, turn, columns),
        )
        return 0

    lax.fori_loop(0, half, one, 0)


def diagonal_group(channels, group, cum_rows, cum_cols, scores, x_ref, writers, readers, out_ref):
    length, heads = cum_cols.shape
    per_group = x_ref.shape[1] // channels
    tile = 128
    sc = lax.dot_general(
        readers, writers, (((1,), (1,)), ((), ())), preferred_element_type=F32
    )
    row = lax.broadcasted_iota(jnp.int32, (length, length), 0)
    col = lax.broadcasted_iota(jnp.int32, (length, length), 1)
    scores[...] = jnp.where(row >= col, sc, 0.0)

    base = pl.multiple_of(group * per_group, per_group)
    rows_all = cum_rows[pl.ds(base, per_group), :]
    cols_all = pltpu.roll(cum_cols[...], heads - base, axis=1)
    starts = list(range(0, length, tile))

    def weights(head, top, bottom):
        column = cols_all[top:bottom, head : head + 1]
        parts = []
        for left in range(0, bottom, tile):
            right = min(left + tile, bottom)
            gap = column - rows_all[head : head + 1, left:right]
            if right > top:
                gap = jnp.minimum(gap, 0.0)
            parts.append((jnp.exp2(gap) * scores[top:bottom, left:right]).astype(BF16))
        return parts[0] if len(parts) == 1 else jnp.concatenate(parts, axis=1)

    lane = lax.broadcasted_iota(jnp.int32, (1, 2 * channels), 1)
    for pair in range(per_group // 2):
        x_pair = x_ref[:, pair * 2 * channels : (pair + 1) * 2 * channels]
        for top in starts:
            bottom = min(top + tile, length)
            both = jnp.concatenate(
                [weights(2 * pair, top, bottom), weights(2 * pair + 1, top, bottom)], axis=0
            )
            mixed = jnp.dot(both, x_pair[:bottom], preferred_element_type=F32)
            out_ref[top:bottom, pair * 2 * channels : (pair + 1) * 2 * channels] = jnp.where(
                lane < channels, mixed[: bottom - top], mixed[bottom - top :]
            )


def diagonals(side, cumulative, inputs, write_vectors, read_vectors):
    length, heads = cumulative.shape
    width = inputs.shape[1]
    padded = -(-length // 128) * 128
    return pl.pallas_call(
        lambda *refs: diagonal_kernel(width // heads, *refs),
        in_specs=[SCALAR] + [WHOLE] * 4,
        out_specs=WHOLE,
        out_shape=jax.ShapeDtypeStruct((length, width // 2), F32),
        scratch_shapes=[
            pltpu.VMEM((heads, padded), F32),
            pltpu.VMEM((length, heads), F32),
            pltpu.VMEM((length, length), F32),
        ],
        compiler_params=pltpu.CompilerParams(vmem_limit_bytes=VMEM_LIMIT),
        cost_estimate=pl.CostEstimate(
            flops=length * length * width,
            bytes_accessed=3 * length * width,
            transcendentals=length * length * heads // 2,
        ),
    )(side, cumulative, inputs, write_vectors, read_vectors)


def scan_kernel(parts, side_ref, term_ref, out_hbm, out_ref, sems):
    along, chip_rows, rows, lanes = out_ref.shape
    rows = rows // 2

    def some(i, states):
        for k in range(along):
            decays = log_decays(term_ref[k, i, 2 * rows :])
            after = []
            for side in range(2):
                span = slice(side * rows, (side + 1) * rows)
                out_ref[k, i, span] = states[side].astype(BF16)
                after.append(jnp.exp(decays[side]) * states[side] + term_ref[k, i, span].astype(F32))
            states = tuple(after)
        return states

    states = (jnp.zeros((rows, lanes), F32),) * 2
    size = chip_rows // parts
    for part in range(parts):
        states = lax.fori_loop(part * size, (part + 1) * size, some, states)
        part_copy(parts, part, out_ref, out_hbm, sems).start()
    for part in range(parts):
        part_copy(parts, part, out_ref, out_hbm, sems).wait()


def entries(side, terms):
    along, chip_rows, rows, lanes = terms.shape
    return off_chip(scan_kernel, (along, chip_rows, rows - EXTRA, lanes), side, terms)


def read_kernel(channels, mine, side_ref, cum_ref, c_ref, diagonal_ref, held_ref, *rest):
    out_hbm, grown_ref, pick_ref, out_ref, sems = rest[-5:]
    half, _, columns = out_ref.shape
    state_size = c_ref.shape[1] // G
    grown_ref[...] = jnp.exp(cum_ref[...])
    pick_ref[...] = head_columns(columns, channels, cum_ref.shape[1])
    blocks_n, blocks_c, rows, lanes = held_ref.shape
    rows = rows // 2
    count = blocks_c // half
    copies = []
    for turn in range(half):
        group = side_ref[0] * half + turn
        decay = spread_heads(grown_ref[...], pick_ref[...], group * (columns // channels))
        readers = group_columns(c_ref, group, state_size)[...]
        if mine:
            readers = jnp.concatenate([readers, readers], axis=1)
        for j in range(count):
            sides = []
            for k in range(2):
                at = turn * count + j
                span = slice(k * rows, (k + 1) * rows)
                held = jnp.concatenate([held_ref[i, at, span] for i in range(blocks_n)], axis=0)
                if mine:
                    came_ref = rest[0]
                    second = side_ref[0] == 1
                    came = jnp.concatenate([came_ref[i, at, span] for i in range(blocks_n)], axis=0)
                    logs = log_decays(came_ref[0, at, 2 * rows :])[k]
                    scale = jnp.exp(jnp.where(second, logs, 0.0))
                    start = scale * held.astype(F32) + jnp.where(second, came.astype(F32), 0.0)
                    held = jnp.concatenate(split_two(start), axis=0)
                sides.append(held)
            read = jnp.dot(readers, jnp.concatenate(sides, axis=1), preferred_element_type=F32)
            span = slice(2 * j * lanes, (2 * j + 2) * lanes)
            wide = slice(turn * columns + 2 * j * lanes, turn * columns + (2 * j + 2) * lanes)
            out_ref[turn, :, span] = (diagonal_ref[:, wide] + read * decay[:, span]).astype(BF16)
        copy = pltpu.make_async_copy(out_ref.at[turn], group_columns(out_hbm, group, columns), sems.at[turn])
        copy.start()
        copies.append(copy)
    for copy in copies:
        copy.wait()


def outputs(side, cumulative, read_vectors, diagonal, held, came=None, done=None):
    length, heads = cumulative.shape
    half = G // 2
    width = diagonal.shape[1] * 2
    columns = width // G
    in_specs = [SCALAR] + [WHOLE] * 4
    args = [side, cumulative, read_vectors, diagonal, held]
    aliases = {}
    if came is not None:
        in_specs.append(WHOLE)
        args.append(came)
    if done is not None:
        in_specs.append(LEFT)
        aliases = {len(args): 0}
        args.append(done)
    return pl.pallas_call(
        lambda *refs: read_kernel(width // heads, came is not None, *refs),
        in_specs=in_specs,
        out_specs=LEFT,
        scratch_shapes=[
            pltpu.VMEM((length, heads), F32),
            pltpu.VMEM((2 * heads, columns), BF16),
            pltpu.VMEM((half, length, columns), BF16),
            pltpu.SemaphoreType.DMA((half,)),
        ],
        out_shape=jax.ShapeDtypeStruct((length, width), BF16),
        input_output_aliases=aliases,
        compiler_params=pltpu.CompilerParams(vmem_limit_bytes=VMEM_LIMIT),
        cost_estimate=pl.CostEstimate(
            flops=2 * length * 128 * width,
            bytes_accessed=2 * length * width,
            transcendentals=0,
        ),
    )(*args)


def shards(inputs, log_decay, write_vectors, read_vectors):
    chips = lax.axis_size("seq") * lax.axis_size("z")
    pieces_n = lax.axis_size("z")
    pieces_c = lax.axis_size("seq")
    own_side = lax.axis_index("c").astype(jnp.int32).reshape(1)
    other_side = 1 - own_side
    swap = [(0, 1), (1, 0)]

    cumulative, gone, inputs, write_vectors = first_states(
        other_side, log_decay, inputs, write_vectors, pieces_n, pieces_c
    )
    came = lax.ppermute(gone, "c", swap)
    kept = second_states(own_side, cumulative, inputs, write_vectors, pieces_n, pieces_c)
    term = joined(own_side, kept, came)

    terms = lax.all_to_all(term.reshape((chips,) + term.shape[2:]), ("z", "seq"), 0, 0, tiled=True)
    diagonal_own = diagonals(own_side, cumulative, inputs, write_vectors, read_vectors)
    terms, diagonal_own = lax.optimization_barrier((terms, diagonal_own))

    held = entries(own_side, terms.reshape(term.shape))
    held = lax.all_to_all(held.reshape((chips,) + held.shape[2:]), ("z", "seq"), 0, 0, tiled=True)
    diagonal_other = diagonals(other_side, cumulative, inputs, write_vectors, read_vectors)
    held, diagonal_other = lax.optimization_barrier((held, diagonal_other))
    held = held.reshape(term.shape[:2] + held.shape[1:])

    held_other = lax.ppermute(given(own_side, held, kept), "c", swap)
    done = outputs(own_side, cumulative, read_vectors, diagonal_own, held, came=came)
    return outputs(other_side, cumulative, read_vectors, diagonal_other, held_other, done=done)


def solution(mesh):
    seq, head = mesh.devices.shape
    fine = Mesh(mesh.devices.reshape(seq, head // 2, 2), ("seq", "z", "c"))
    spec = P(("seq", "z", "c"), None)
    return jax.shard_map(
        shards, mesh=fine, in_specs=(spec,) * 4, out_specs=spec, check_vma=False
    )
```

```python
import functools
import math

import jax
import jax.numpy as jnp
from jax import lax
from jax.experimental import pallas as pl
from jax.experimental.pallas import tpu as pltpu
from jax.sharding import Mesh, PartitionSpec as P

G = 8
LOG2E = math.log2(math.e)
VMEM_LIMIT = 16 * 1024 * 1024
EXTRA = 8
THIN = 4
F32 = jnp.float32
BF16 = jnp.bfloat16


def split_two(a):
    high = a.astype(BF16)
    return high, (a - high.astype(F32)).astype(BF16)


def split_three(a):
    high = a.astype(BF16)
    rest = a - high.astype(F32)
    middle, low = split_two(rest)
    return high, middle, low


def head_columns(columns, channels, heads):
    row = lax.broadcasted_iota(jnp.int32, (heads, columns), 0)
    col = lax.broadcasted_iota(jnp.int32, (heads, columns), 1)
    shift = channels.bit_length() - 1
    pick = jnp.where(row == lax.shift_right_logical(col, shift), 1.0, 0.0).astype(BF16)
    return jnp.concatenate([pick, pick], axis=0)


def spread_heads(values, pick, base):
    values = pltpu.roll(values, values.shape[1] - base, axis=1)
    high, low = split_two(values)
    return jnp.dot(jnp.concatenate([high, low], axis=1), pick, preferred_element_type=F32)


def group_columns(ref, group, columns):
    return ref.at[:, pl.ds(pl.multiple_of(group * columns, columns), columns)]


def decay_rows(total, pick, base):
    heads = total.shape[1]
    total = pltpu.roll(jnp.broadcast_to(total, (EXTRA, heads)), heads - base, axis=1)
    high, middle, low = (part.astype(F32) for part in split_three(total))
    row = lax.broadcasted_iota(jnp.int32, (EXTRA, heads), 0)
    sides = []
    for start in (0, 3):
        rows = jnp.where(row == start, high, jnp.where(row == start + 1, middle, jnp.where(row == start + 2, low, 0.0)))
        sides.append(jnp.dot(rows.astype(BF16), pick[:heads], preferred_element_type=F32))
    return sides


def log_decays(rows):
    rows = rows.astype(F32)
    return tuple(rows[i + 2 : i + 3] + rows[i + 1 : i + 2] + rows[i : i + 1] for i in (0, 3))


def pack_decays(first, second):
    parts = [part.astype(F32) for whole in (first, second) for part in split_two(whole)]
    return jnp.concatenate(parts, axis=0).astype(BF16)


def running_sum(a):
    length = a.shape[0]
    row = lax.broadcasted_iota(jnp.int32, (length, length), 0)
    col = lax.broadcasted_iota(jnp.int32, (length, length), 1)
    lower = jnp.where(row >= col, 1.0, 0.0).astype(BF16)
    high, middle, low = split_three(a)
    return (
        jnp.dot(lower, low, preferred_element_type=F32)
        + jnp.dot(lower, middle, preferred_element_type=F32)
        + jnp.dot(lower, high, preferred_element_type=F32)
    )


def write_group(channels, group, turn, x, writers, fade, total, pick, state_ref):
    columns = x.shape[1]
    base = group * (columns // channels)
    high, low = split_two(x.astype(F32) * spread_heads(fade, pick, base))
    state = lax.dot_general(
        jnp.concatenate([writers, writers], axis=0),
        jnp.concatenate([high, low], axis=0),
        (((0,), (0,)), ((), ())),
        preferred_element_type=F32,
    ).astype(BF16)
    decays = decay_rows(total, pick, base)
    blocks_n, blocks_c, rows, lanes = state_ref.shape
    rows = (rows - EXTRA) // 2
    count = columns // lanes // 2
    for j in range(count):
        left, middle, right = (k * lanes for k in (2 * j, 2 * j + 1, 2 * j + 2))
        extra = (decays[0][:, left:middle] + decays[1][:, middle:right]).astype(BF16)
        for i in range(blocks_n):
            span = slice(i * rows, (i + 1) * rows)
            state_ref[i, turn * count + j, :rows] = state[span, left:middle]
            state_ref[i, turn * count + j, rows : 2 * rows] = state[span, middle:right]
            state_ref[i, turn * count + j, 2 * rows :] = extra


def first_kernel(channels, side_ref, a_hbm, x_hbm, b_hbm, cum_ref, state_ref, x_ref, b_ref, fade_ref, pick_ref, a_sem, x_sems, b_sems):
    columns = x_ref.shape[1] // G
    state_size = b_ref.shape[1] // G
    half = G // 2
    length, heads = cum_ref.shape
    bring = pltpu.make_async_copy(a_hbm, cum_ref, a_sem)
    bring.start()
    copies = []
    for turn in range(G):
        side = side_ref[0] if turn < half else 1 - side_ref[0]
        group = side * half + turn % half
        pair = (
            pltpu.make_async_copy(
                group_columns(b_hbm, group, state_size), group_columns(b_ref, group, state_size), b_sems.at[turn]
            ),
            pltpu.make_async_copy(
                group_columns(x_hbm, group, columns), group_columns(x_ref, group, columns), x_sems.at[turn]
            ),
        )
        for copy in pair:
            copy.start()
        copies.append((group, pair))
    pick = head_columns(columns, channels, heads)
    bring.wait()
    cum = running_sum(cum_ref[...])
    cum_ref[...] = cum
    total = cum[length - 1 :, :]
    fade_ref[...] = jnp.exp(jnp.minimum(total - cum, 0.0))
    pick_ref[...] = pick
    for turn, (group, pair) in enumerate(copies):
        for copy in pair:
            copy.wait()
        if turn < half:
            write_group(
                channels, group, turn,
                group_columns(x_ref, group, columns)[...],
                group_columns(b_ref, group, state_size)[...],
                fade_ref[...], total, pick_ref[...], state_ref,
            )


def second_kernel(channels, side_ref, cum_ref, x_ref, b_ref, state_ref, fade_ref, pick_ref):
    columns = x_ref.shape[1] // G
    state_size = b_ref.shape[1] // G
    half = G // 2
    length, heads = cum_ref.shape
    cum = cum_ref[...]
    total = cum[length - 1 :, :]
    fade_ref[...] = jnp.exp(jnp.minimum(total - cum, 0.0))
    pick_ref[...] = head_columns(columns, channels, heads)
    for turn in range(half):
        group = side_ref[0] * half + turn
        write_group(
            channels, group, turn,
            group_columns(x_ref, group, columns)[...],
            group_columns(b_ref, group, state_size)[...],
            fade_ref[...], total, pick_ref[...], state_ref,
        )


WHOLE = pl.BlockSpec(memory_space=pltpu.VMEM)
SCALAR = pl.BlockSpec(memory_space=pltpu.SMEM)
LEFT = pl.BlockSpec(memory_space=pltpu.HBM)


def state_shape(length, width, state_size, pieces_n, pieces_c):
    lanes = width // 2 // pieces_c // 2
    return jax.ShapeDtypeStruct((pieces_n, pieces_c, 2 * state_size // pieces_n + EXTRA, lanes), BF16)


def first_states(side, log_decay, inputs, write_vectors, pieces_n, pieces_c):
    length, heads = log_decay.shape
    width = inputs.shape[1]
    return pl.pallas_call(
        lambda *refs: first_kernel(width // heads, *refs),
        in_specs=[SCALAR, LEFT, LEFT, LEFT],
        out_specs=[WHOLE] * 4,
        out_shape=[
            jax.ShapeDtypeStruct(log_decay.shape, F32),
            state_shape(length, width, write_vectors.shape[1] // G, pieces_n, pieces_c),
            jax.ShapeDtypeStruct(inputs.shape, BF16),
            jax.ShapeDtypeStruct(write_vectors.shape, BF16),
        ],
        scratch_shapes=[
            pltpu.VMEM((length, heads), F32),
            pltpu.VMEM((2 * heads, width // G), BF16),
            pltpu.SemaphoreType.DMA,
            pltpu.SemaphoreType.DMA((G,)),
            pltpu.SemaphoreType.DMA((G,)),
        ],
        compiler_params=pltpu.CompilerParams(vmem_limit_bytes=VMEM_LIMIT),
        cost_estimate=pl.CostEstimate(flops=2 * length * 256 * width, bytes_accessed=4 * inputs.size, transcendentals=0),
    )(side, *(pltpu.with_memory_space_constraint(a, pltpu.HBM) for a in (log_decay, inputs, write_vectors)))


def second_states(side, cumulative, inputs, write_vectors, pieces_n, pieces_c):
    length, heads = cumulative.shape
    width = inputs.shape[1]
    return pl.pallas_call(
        lambda *refs: second_kernel(width // heads, *refs),
        in_specs=[SCALAR, WHOLE, WHOLE, WHOLE],
        out_specs=WHOLE,
        out_shape=state_shape(length, width, write_vectors.shape[1] // G, pieces_n, pieces_c),
        scratch_shapes=[pltpu.VMEM((length, heads), F32), pltpu.VMEM((2 * heads, width // G), BF16)],
        compiler_params=pltpu.CompilerParams(vmem_limit_bytes=VMEM_LIMIT),
        cost_estimate=pl.CostEstimate(flops=2 * length * 256 * width, bytes_accessed=inputs.size, transcendentals=0),
    )(side, cumulative, inputs, write_vectors)


def join_kernel(parts, side_ref, kept_ref, came_ref, out_hbm, out_ref, sems):
    blocks_n, blocks_c, rows, _ = kept_ref.shape
    rows = (rows - EXTRA) // 2

    def join(first_ref, second_ref):
        for j in range(blocks_c):
            before = log_decays(first_ref[0, j, 2 * rows :])
            after = log_decays(second_ref[0, j, 2 * rows :])
            extra = pack_decays(*(a + b for a, b in zip(before, after)))
            for k in range(2):
                span = slice(k * rows, (k + 1) * rows)
                decay = jnp.exp(after[k])
                for i in range(blocks_n):
                    both = decay * first_ref[i, j, span].astype(F32) + second_ref[i, j, span].astype(F32)
                    for r in range(rows // THIN):
                        thin = both[r * THIN : (r + 1) * THIN]
                        out_ref[i, j, k * (rows // THIN) + r] = thin.astype(BF16)
            for i in range(blocks_n):
                out_ref[i, j, 2 * rows // THIN] = extra
            if (j + 1) % (blocks_c // parts) == 0:
                part_copy(parts, j * parts // blocks_c, out_ref, out_hbm, sems).start()

    @pl.when(side_ref[0] == 0)
    def _():
        join(kept_ref, came_ref)

    @pl.when(side_ref[0] == 1)
    def _():
        join(came_ref, kept_ref)

    for part in range(parts):
        part_copy(parts, part, out_ref, out_hbm, sems).wait()


def on_chip(kernel, shape, side, *arrays):
    whole = pl.BlockSpec(memory_space=pltpu.VMEM)
    return pl.pallas_call(
        kernel,
        in_specs=[pl.BlockSpec(memory_space=pltpu.SMEM)] + [whole] * len(arrays),
        out_specs=whole,
        out_shape=jax.ShapeDtypeStruct(shape, BF16),
        compiler_params=pltpu.CompilerParams(vmem_limit_bytes=VMEM_LIMIT),
    )(side, *arrays)


def off_chip(kernel, shape, side, *arrays):
    parts = 4
    whole = pl.BlockSpec(memory_space=pltpu.VMEM)
    return pl.pallas_call(
        functools.partial(kernel, parts),
        in_specs=[pl.BlockSpec(memory_space=pltpu.SMEM)] + [whole] * len(arrays),
        out_specs=LEFT,
        out_shape=pltpu.HBM(shape, BF16),
        scratch_shapes=[pltpu.VMEM(shape, BF16), pltpu.SemaphoreType.DMA((parts,))],
        compiler_params=pltpu.CompilerParams(vmem_limit_bytes=VMEM_LIMIT),
    )(side, *arrays)


def part_copy(parts, part, out_ref, out_hbm, sems):
    size = out_ref.shape[1] // parts
    span = pl.ds(part * size, size)
    return pltpu.make_async_copy(out_ref.at[:, span], out_hbm.at[:, span], sems.at[part])


def joined(side, kept, came):
    blocks_n, blocks_c, rows, lanes = kept.shape
    shape = (blocks_n, blocks_c, (rows - EXTRA) // THIN + 1, THIN, lanes)
    return off_chip(join_kernel, shape, side, kept, came)


def give_kernel(side_ref, held_ref, kept_ref, out_ref):
    blocks_n, blocks_c, rows, _ = held_ref.shape
    rows = rows // 2

    @pl.when(side_ref[0] == 0)
    def _():
        for j in range(blocks_c):
            logs = log_decays(kept_ref[0, j, 2 * rows :])
            for k in range(2):
                span = slice(k * rows, (k + 1) * rows)
                decay = jnp.exp(logs[k])
                for i in range(blocks_n):
                    out_ref[i, j, span] = (
                        decay * held_ref[i, j, span].astype(F32) + kept_ref[i, j, span].astype(F32)
                    ).astype(BF16)

    @pl.when(side_ref[0] == 1)
    def _():
        out_ref[...] = held_ref[...]


def given(side, held, kept):
    return on_chip(give_kernel, held.shape, side, held, kept)


def diagonal_kernel(channels, side_ref, cum_ref, x_ref, b_ref, c_ref, out_ref, cum_rows, cum_cols, scores):
    length, heads = cum_ref.shape
    columns = x_ref.shape[1] // G
    state_size = b_ref.shape[1] // G
    per_group = columns // channels
    half = G // 2
    padded = cum_rows.shape[1]

    scaled = cum_ref[...] * LOG2E
    cum_cols[...] = scaled
    tall = jnp.concatenate([scaled, jnp.zeros((padded - length, heads), F32)], axis=0)
    cum_rows[...] = tall.T

    def one(turn, _):
        group = turn + side_ref[0] * half
        diagonal_group(
            channels, group, cum_rows, cum_cols, scores,
            group_columns(x_ref, group, columns),
            group_columns(b_ref, group, state_size)[...],
            group_columns(c_ref, group, state_size)[...],
            group_columns(out_ref, turn, columns),
        )
        return 0

    lax.fori_loop(0, half, one, 0)


def diagonal_group(channels, group, cum_rows, cum_cols, scores, x_ref, writers, readers, out_ref):
    length, heads = cum_cols.shape
    per_group = x_ref.shape[1] // channels
    tile = 128
    sc = lax.dot_general(
        readers, writers, (((1,), (1,)), ((), ())), preferred_element_type=F32
    )
    row = lax.broadcasted_iota(jnp.int32, (length, length), 0)
    col = lax.broadcasted_iota(jnp.int32, (length, length), 1)
    scores[...] = jnp.where(row >= col, sc, 0.0)

    base = pl.multiple_of(group * per_group, per_group)
    rows_all = cum_rows[pl.ds(base, per_group), :]
    cols_all = pltpu.roll(cum_cols[...], heads - base, axis=1)
    starts = list(range(0, length, tile))

    def weights(head, top, bottom):
        column = cols_all[top:bottom, head : head + 1]
        parts = []
        for left in range(0, bottom, tile):
            right = min(left + tile, bottom)
            gap = column - rows_all[head : head + 1, left:right]
            if right > top:
                gap = jnp.minimum(gap, 0.0)
            parts.append((jnp.exp2(gap) * scores[top:bottom, left:right]).astype(BF16))
        return parts[0] if len(parts) == 1 else jnp.concatenate(parts, axis=1)

    lane = lax.broadcasted_iota(jnp.int32, (1, 2 * channels), 1)
    for pair in range(per_group // 2):
        x_pair = x_ref[:, pair * 2 * channels : (pair + 1) * 2 * channels]
        for top in starts:
            bottom = min(top + tile, length)
            both = jnp.concatenate(
                [weights(2 * pair, top, bottom), weights(2 * pair + 1, top, bottom)], axis=0
            )
            mixed = jnp.dot(both, x_pair[:bottom], preferred_element_type=F32)
            out_ref[top:bottom, pair * 2 * channels : (pair + 1) * 2 * channels] = jnp.where(
                lane < channels, mixed[: bottom - top], mixed[bottom - top :]
            )


def diagonals(side, cumulative, inputs, write_vectors, read_vectors):
    length, heads = cumulative.shape
    width = inputs.shape[1]
    padded = -(-length // 128) * 128
    return pl.pallas_call(
        lambda *refs: diagonal_kernel(width // heads, *refs),
        in_specs=[SCALAR] + [WHOLE] * 4,
        out_specs=WHOLE,
        out_shape=jax.ShapeDtypeStruct((length, width // 2), F32),
        scratch_shapes=[
            pltpu.VMEM((heads, padded), F32),
            pltpu.VMEM((length, heads), F32),
            pltpu.VMEM((length, length), F32),
        ],
        compiler_params=pltpu.CompilerParams(vmem_limit_bytes=VMEM_LIMIT),
        cost_estimate=pl.CostEstimate(
            flops=length * length * width,
            bytes_accessed=3 * length * width,
            transcendentals=length * length * heads // 2,
        ),
    )(side, cumulative, inputs, write_vectors, read_vectors)


def scan_kernel(parts, side_ref, term_ref, out_hbm, out_ref, sems):
    along, chip_rows, rows, lanes = out_ref.shape
    rows = rows // 2

    def some(i, states):
        for k in range(along):
            logs = term_ref[k, i, 2 * rows // THIN].astype(F32)
            after = []
            for side in range(2):
                span = slice(side * rows, (side + 1) * rows)
                out_ref[k, i, span] = states[side].astype(BF16)
                decay = jnp.exp(logs[2 * side : 2 * side + 1] + logs[2 * side + 1 : 2 * side + 2])
                first = side * (rows // THIN)
                term = [term_ref[k, i, first + r].astype(F32) for r in range(rows // THIN)]
                after.append(decay * states[side] + jnp.concatenate(term, axis=0))
            states = tuple(after)
        return states

    states = (jnp.zeros((rows, lanes), F32),) * 2
    size = chip_rows // parts
    for part in range(parts):
        states = lax.fori_loop(part * size, (part + 1) * size, some, states)
        part_copy(parts, part, out_ref, out_hbm, sems).start()
    for part in range(parts):
        part_copy(parts, part, out_ref, out_hbm, sems).wait()


def entries(side, terms):
    along, chip_rows, thins, _, lanes = terms.shape
    return off_chip(scan_kernel, (along, chip_rows, (thins - 1) * THIN, lanes), side, terms)


def read_kernel(channels, mine, side_ref, cum_ref, c_ref, diagonal_ref, held_ref, *rest):
    out_hbm, grown_ref, pick_ref, out_ref, sems = rest[-5:]
    half, _, columns = out_ref.shape
    state_size = c_ref.shape[1] // G
    grown_ref[...] = jnp.exp(cum_ref[...])
    pick_ref[...] = head_columns(columns, channels, cum_ref.shape[1])
    blocks_n, blocks_c, rows, lanes = held_ref.shape
    rows = rows // 2
    count = blocks_c // half
    copies = []
    for turn in range(half):
        group = side_ref[0] * half + turn
        decay = spread_heads(grown_ref[...], pick_ref[...], group * (columns // channels))
        readers = group_columns(c_ref, group, state_size)[...]
        if mine:
            readers = jnp.concatenate([readers, readers], axis=1)
        for j in range(count):
            sides = []
            for k in range(2):
                at = turn * count + j
                span = slice(k * rows, (k + 1) * rows)
                held = jnp.concatenate([held_ref[i, at, span] for i in range(blocks_n)], axis=0)
                if mine:
                    came_ref = rest[0]
                    second = side_ref[0] == 1
                    came = jnp.concatenate([came_ref[i, at, span] for i in range(blocks_n)], axis=0)
                    logs = log_decays(came_ref[0, at, 2 * rows :])[k]
                    scale = jnp.exp(jnp.where(second, logs, 0.0))
                    start = scale * held.astype(F32) + jnp.where(second, came.astype(F32), 0.0)
                    held = jnp.concatenate(split_two(start), axis=0)
                sides.append(held)
            read = jnp.dot(readers, jnp.concatenate(sides, axis=1), preferred_element_type=F32)
            span = slice(2 * j * lanes, (2 * j + 2) * lanes)
            wide = slice(turn * columns + 2 * j * lanes, turn * columns + (2 * j + 2) * lanes)
            out_ref[turn, :, span] = (diagonal_ref[:, wide] + read * decay[:, span]).astype(BF16)
        copy = pltpu.make_async_copy(out_ref.at[turn], group_columns(out_hbm, group, columns), sems.at[turn])
        copy.start()
        copies.append(copy)
    for copy in copies:
        copy.wait()


def outputs(side, cumulative, read_vectors, diagonal, held, came=None, done=None):
    length, heads = cumulative.shape
    half = G // 2
    width = diagonal.shape[1] * 2
    columns = width // G
    in_specs = [SCALAR] + [WHOLE] * 4
    args = [side, cumulative, read_vectors, diagonal, held]
    aliases = {}
    if came is not None:
        in_specs.append(WHOLE)
        args.append(came)
    if done is not None:
        in_specs.append(LEFT)
        aliases = {len(args): 0}
        args.append(done)
    return pl.pallas_call(
        lambda *refs: read_kernel(width // heads, came is not None, *refs),
        in_specs=in_specs,
        out_specs=LEFT,
        scratch_shapes=[
            pltpu.VMEM((length, heads), F32),
            pltpu.VMEM((2 * heads, columns), BF16),
            pltpu.VMEM((half, length, columns), BF16),
            pltpu.SemaphoreType.DMA((half,)),
        ],
        out_shape=jax.ShapeDtypeStruct((length, width), BF16),
        input_output_aliases=aliases,
        compiler_params=pltpu.CompilerParams(vmem_limit_bytes=VMEM_LIMIT),
        cost_estimate=pl.CostEstimate(
            flops=2 * length * 128 * width,
            bytes_accessed=2 * length * width,
            transcendentals=0,
        ),
    )(*args)


def shards(inputs, log_decay, write_vectors, read_vectors):
    chips = lax.axis_size("seq") * lax.axis_size("z")
    pieces_n = lax.axis_size("z")
    pieces_c = lax.axis_size("seq")
    own_side = lax.axis_index("c").astype(jnp.int32).reshape(1)
    other_side = 1 - own_side
    swap = [(0, 1), (1, 0)]

    cumulative, gone, inputs, write_vectors = first_states(
        other_side, log_decay, inputs, write_vectors, pieces_n, pieces_c
    )
    came = lax.ppermute(gone, "c", swap)
    kept = second_states(own_side, cumulative, inputs, write_vectors, pieces_n, pieces_c)
    term = joined(own_side, kept, came)

    terms = lax.all_to_all(term.reshape((chips,) + term.shape[2:]), ("z", "seq"), 0, 0, tiled=True)
    diagonal_own = diagonals(own_side, cumulative, inputs, write_vectors, read_vectors)
    terms, diagonal_own = lax.optimization_barrier((terms, diagonal_own))

    held = entries(own_side, terms.reshape(term.shape))
    held = lax.all_to_all(held.reshape((chips,) + held.shape[2:]), ("z", "seq"), 0, 0, tiled=True)
    diagonal_other = diagonals(other_side, cumulative, inputs, write_vectors, read_vectors)
    held, diagonal_other = lax.optimization_barrier((held, diagonal_other))
    held = held.reshape(term.shape[:2] + held.shape[1:])

    held_other = lax.ppermute(given(own_side, held, kept), "c", swap)
    done = outputs(own_side, cumulative, read_vectors, diagonal_own, held, came=came)
    return outputs(other_side, cumulative, read_vectors, diagonal_other, held_other, done=done)


def solution(mesh):
    seq, head = mesh.devices.shape
    fine = Mesh(mesh.devices.reshape(seq, head // 2, 2), ("seq", "z", "c"))
    spec = P(("seq", "z", "c"), None)
    return jax.shard_map(
        shards, mesh=fine, in_specs=(spec,) * 4, out_specs=spec, check_vma=False
    )
```

```python
import functools
import math

import jax
import jax.numpy as jnp
from jax import lax
from jax.experimental import pallas as pl
from jax.experimental.pallas import tpu as pltpu
from jax.sharding import Mesh, PartitionSpec as P

G = 8
LOG2E = math.log2(math.e)
VMEM_LIMIT = 16 * 1024 * 1024
EXTRA = 8
THIN = 4
F32 = jnp.float32
BF16 = jnp.bfloat16


def split_two(a):
    high = a.astype(BF16)
    return high, (a - high.astype(F32)).astype(BF16)


def split_three(a):
    high = a.astype(BF16)
    rest = a - high.astype(F32)
    middle, low = split_two(rest)
    return high, middle, low


def head_columns(columns, channels, heads):
    row = lax.broadcasted_iota(jnp.int32, (heads, columns), 0)
    col = lax.broadcasted_iota(jnp.int32, (heads, columns), 1)
    shift = channels.bit_length() - 1
    pick = jnp.where(row == lax.shift_right_logical(col, shift), 1.0, 0.0).astype(BF16)
    return jnp.concatenate([pick, pick], axis=0)


def spread_heads(values, pick, base):
    values = pltpu.roll(values, values.shape[1] - base, axis=1)
    high, low = split_two(values)
    return jnp.dot(jnp.concatenate([high, low], axis=1), pick, preferred_element_type=F32)


def group_columns(ref, group, columns):
    return ref.at[:, pl.ds(pl.multiple_of(group * columns, columns), columns)]


def decay_rows(total, pick, base):
    heads = total.shape[1]
    total = pltpu.roll(jnp.broadcast_to(total, (EXTRA, heads)), heads - base, axis=1)
    high, middle, low = (part.astype(F32) for part in split_three(total))
    row = lax.broadcasted_iota(jnp.int32, (EXTRA, heads), 0)
    sides = []
    for start in (0, 3):
        rows = jnp.where(row == start, high, jnp.where(row == start + 1, middle, jnp.where(row == start + 2, low, 0.0)))
        sides.append(jnp.dot(rows.astype(BF16), pick[:heads], preferred_element_type=F32))
    return sides


def log_decays(rows):
    rows = rows.astype(F32)
    return tuple(rows[i + 2 : i + 3] + rows[i + 1 : i + 2] + rows[i : i + 1] for i in (0, 3))


def pack_decays(first, second):
    parts = [part.astype(F32) for whole in (first, second) for part in split_two(whole)]
    return jnp.concatenate(parts, axis=0).astype(BF16)


def running_sum(a):
    length = a.shape[0]
    row = lax.broadcasted_iota(jnp.int32, (length, length), 0)
    col = lax.broadcasted_iota(jnp.int32, (length, length), 1)
    lower = jnp.where(row >= col, 1.0, 0.0).astype(BF16)
    high, middle, low = split_three(a)
    return (
        jnp.dot(lower, low, preferred_element_type=F32)
        + jnp.dot(lower, middle, preferred_element_type=F32)
        + jnp.dot(lower, high, preferred_element_type=F32)
    )


def write_group(channels, group, turn, x, writers, fade, total, pick, state_ref):
    columns = x.shape[1]
    base = group * (columns // channels)
    high, low = split_two(x.astype(F32) * spread_heads(fade, pick, base))
    state = lax.dot_general(
        jnp.concatenate([writers, writers], axis=0),
        jnp.concatenate([high, low], axis=0),
        (((0,), (0,)), ((), ())),
        preferred_element_type=F32,
    ).astype(BF16)
    decays = decay_rows(total, pick, base)
    blocks_n, blocks_c, rows, lanes = state_ref.shape
    rows = (rows - EXTRA) // 2
    count = columns // lanes // 2
    for j in range(count):
        left, middle, right = (k * lanes for k in (2 * j, 2 * j + 1, 2 * j + 2))
        extra = (decays[0][:, left:middle] + decays[1][:, middle:right]).astype(BF16)
        for i in range(blocks_n):
            span = slice(i * rows, (i + 1) * rows)
            state_ref[i, turn * count + j, :rows] = state[span, left:middle]
            state_ref[i, turn * count + j, rows : 2 * rows] = state[span, middle:right]
            state_ref[i, turn * count + j, 2 * rows :] = extra


def first_kernel(channels, side_ref, a_hbm, x_hbm, b_hbm, cum_ref, state_ref, x_ref, b_ref, fade_ref, pick_ref, a_sem, x_sems, b_sems):
    columns = x_ref.shape[1] // G
    state_size = b_ref.shape[1] // G
    half = G // 2
    length, heads = cum_ref.shape
    bring = pltpu.make_async_copy(a_hbm, cum_ref, a_sem)
    bring.start()
    copies = []
    for turn in range(G):
        side = side_ref[0] if turn < half else 1 - side_ref[0]
        group = side * half + turn % half
        pair = (
            pltpu.make_async_copy(
                group_columns(b_hbm, group, state_size), group_columns(b_ref, group, state_size), b_sems.at[turn]
            ),
            pltpu.make_async_copy(
                group_columns(x_hbm, group, columns), group_columns(x_ref, group, columns), x_sems.at[turn]
            ),
        )
        for copy in pair:
            copy.start()
        copies.append((group, pair))
    pick = head_columns(columns, channels, heads)
    bring.wait()
    cum = running_sum(cum_ref[...])
    cum_ref[...] = cum
    total = cum[length - 1 :, :]
    fade_ref[...] = jnp.exp(jnp.minimum(total - cum, 0.0))
    pick_ref[...] = pick
    for turn, (group, pair) in enumerate(copies):
        for copy in pair:
            copy.wait()
        if turn < half:
            write_group(
                channels, group, turn,
                group_columns(x_ref, group, columns)[...],
                group_columns(b_ref, group, state_size)[...],
                fade_ref[...], total, pick_ref[...], state_ref,
            )


def second_kernel(channels, side_ref, cum_ref, x_ref, b_ref, state_ref, fade_ref, pick_ref):
    columns = x_ref.shape[1] // G
    state_size = b_ref.shape[1] // G
    half = G // 2
    length, heads = cum_ref.shape
    cum = cum_ref[...]
    total = cum[length - 1 :, :]
    fade_ref[...] = jnp.exp(jnp.minimum(total - cum, 0.0))
    pick_ref[...] = head_columns(columns, channels, heads)
    for turn in range(half):
        group = side_ref[0] * half + turn
        write_group(
            channels, group, turn,
            group_columns(x_ref, group, columns)[...],
            group_columns(b_ref, group, state_size)[...],
            fade_ref[...], total, pick_ref[...], state_ref,
        )


WHOLE = pl.BlockSpec(memory_space=pltpu.VMEM)
SCALAR = pl.BlockSpec(memory_space=pltpu.SMEM)
LEFT = pl.BlockSpec(memory_space=pltpu.HBM)


def state_shape(length, width, state_size, pieces_n, pieces_c):
    lanes = width // 2 // pieces_c // 2
    return jax.ShapeDtypeStruct((pieces_n, pieces_c, 2 * state_size // pieces_n + EXTRA, lanes), BF16)


def first_states(side, log_decay, inputs, write_vectors, pieces_n, pieces_c):
    length, heads = log_decay.shape
    width = inputs.shape[1]
    return pl.pallas_call(
        lambda *refs: first_kernel(width // heads, *refs),
        in_specs=[SCALAR, LEFT, LEFT, LEFT],
        out_specs=[WHOLE] * 4,
        out_shape=[
            jax.ShapeDtypeStruct(log_decay.shape, F32),
            state_shape(length, width, write_vectors.shape[1] // G, pieces_n, pieces_c),
            jax.ShapeDtypeStruct(inputs.shape, BF16),
            jax.ShapeDtypeStruct(write_vectors.shape, BF16),
        ],
        scratch_shapes=[
            pltpu.VMEM((length, heads), F32),
            pltpu.VMEM((2 * heads, width // G), BF16),
            pltpu.SemaphoreType.DMA,
            pltpu.SemaphoreType.DMA((G,)),
            pltpu.SemaphoreType.DMA((G,)),
        ],
        compiler_params=pltpu.CompilerParams(vmem_limit_bytes=VMEM_LIMIT),
        cost_estimate=pl.CostEstimate(flops=2 * length * 256 * width, bytes_accessed=4 * inputs.size, transcendentals=0),
    )(side, *(pltpu.with_memory_space_constraint(a, pltpu.HBM) for a in (log_decay, inputs, write_vectors)))


def second_states(side, cumulative, inputs, write_vectors, pieces_n, pieces_c):
    length, heads = cumulative.shape
    width = inputs.shape[1]
    return pl.pallas_call(
        lambda *refs: second_kernel(width // heads, *refs),
        in_specs=[SCALAR, WHOLE, WHOLE, WHOLE],
        out_specs=WHOLE,
        out_shape=state_shape(length, width, write_vectors.shape[1] // G, pieces_n, pieces_c),
        scratch_shapes=[pltpu.VMEM((length, heads), F32), pltpu.VMEM((2 * heads, width // G), BF16)],
        compiler_params=pltpu.CompilerParams(vmem_limit_bytes=VMEM_LIMIT),
        cost_estimate=pl.CostEstimate(flops=2 * length * 256 * width, bytes_accessed=inputs.size, transcendentals=0),
    )(side, cumulative, inputs, write_vectors)


def join_kernel(parts, side_ref, kept_ref, came_ref, out_hbm, out_ref, sems):
    blocks_n, blocks_c, rows, _ = kept_ref.shape
    rows = (rows - EXTRA) // 2

    def join(first_ref, second_ref):
        for j in range(blocks_c):
            before = log_decays(first_ref[0, j, 2 * rows :])
            after = log_decays(second_ref[0, j, 2 * rows :])
            extra = pack_decays(*(a + b for a, b in zip(before, after)))
            for k in range(2):
                span = slice(k * rows, (k + 1) * rows)
                decay = jnp.exp(after[k])
                for i in range(blocks_n):
                    both = decay * first_ref[i, j, span].astype(F32) + second_ref[i, j, span].astype(F32)
                    for r in range(rows // THIN):
                        thin = both[r * THIN : (r + 1) * THIN]
                        out_ref[i, j, k * (rows // THIN) + r] = thin.astype(BF16)
            for i in range(blocks_n):
                out_ref[i, j, 2 * rows // THIN] = extra
            if (j + 1) % (blocks_c // parts) == 0:
                part_copy(parts, j * parts // blocks_c, out_ref, out_hbm, sems).start()

    @pl.when(side_ref[0] == 0)
    def _():
        join(kept_ref, came_ref)

    @pl.when(side_ref[0] == 1)
    def _():
        join(came_ref, kept_ref)

    for part in range(parts):
        part_copy(parts, part, out_ref, out_hbm, sems).wait()


def on_chip(kernel, shape, side, *arrays):
    whole = pl.BlockSpec(memory_space=pltpu.VMEM)
    return pl.pallas_call(
        kernel,
        in_specs=[pl.BlockSpec(memory_space=pltpu.SMEM)] + [whole] * len(arrays),
        out_specs=whole,
        out_shape=jax.ShapeDtypeStruct(shape, BF16),
        compiler_params=pltpu.CompilerParams(vmem_limit_bytes=VMEM_LIMIT),
    )(side, *arrays)


def off_chip(kernel, shape, side, *arrays):
    parts = 4
    whole = pl.BlockSpec(memory_space=pltpu.VMEM)
    return pl.pallas_call(
        functools.partial(kernel, parts),
        in_specs=[pl.BlockSpec(memory_space=pltpu.SMEM)] + [whole] * len(arrays),
        out_specs=LEFT,
        out_shape=pltpu.HBM(shape, BF16),
        scratch_shapes=[pltpu.VMEM(shape, BF16), pltpu.SemaphoreType.DMA((parts,))],
        compiler_params=pltpu.CompilerParams(vmem_limit_bytes=VMEM_LIMIT),
    )(side, *arrays)


def part_copy(parts, part, out_ref, out_hbm, sems):
    size = out_ref.shape[1] // parts
    span = pl.ds(part * size, size)
    return pltpu.make_async_copy(out_ref.at[:, span], out_hbm.at[:, span], sems.at[part])


def joined(side, kept, came):
    blocks_n, blocks_c, rows, lanes = kept.shape
    shape = (blocks_n, blocks_c, (rows - EXTRA) // THIN + 1, THIN, lanes)
    return off_chip(join_kernel, shape, side, kept, came)


def give_kernel(side_ref, held_ref, kept_ref, out_ref):
    blocks_n, blocks_c, rows, _ = held_ref.shape
    rows = rows // 2

    @pl.when(side_ref[0] == 0)
    def _():
        for j in range(blocks_c):
            logs = log_decays(kept_ref[0, j, 2 * rows :])
            for k in range(2):
                span = slice(k * rows, (k + 1) * rows)
                decay = jnp.exp(logs[k])
                for i in range(blocks_n):
                    out_ref[i, j, span] = (
                        decay * held_ref[i, j, span].astype(F32) + kept_ref[i, j, span].astype(F32)
                    ).astype(BF16)

    @pl.when(side_ref[0] == 1)
    def _():
        out_ref[...] = held_ref[...]


def given(side, held, kept):
    return on_chip(give_kernel, held.shape, side, held, kept)


def diagonal_kernel(channels, side_ref, cum_ref, x_ref, b_ref, c_ref, out_ref, cum_rows, cum_cols, scores):
    length, heads = cum_ref.shape
    columns = x_ref.shape[1] // G
    state_size = b_ref.shape[1] // G
    per_group = columns // channels
    half = G // 2
    padded = cum_rows.shape[1]

    scaled = cum_ref[...] * LOG2E
    cum_cols[...] = scaled
    tall = jnp.concatenate([scaled, jnp.zeros((padded - length, heads), F32)], axis=0)
    cum_rows[...] = tall.T

    def one(turn, _):
        group = turn + side_ref[0] * half
        diagonal_group(
            channels, group, cum_rows, cum_cols, scores,
            group_columns(x_ref, group, columns),
            group_columns(b_ref, group, state_size)[...],
            group_columns(c_ref, group, state_size)[...],
            group_columns(out_ref, turn, columns),
        )
        return 0

    lax.fori_loop(0, half, one, 0)


def diagonal_group(channels, group, cum_rows, cum_cols, scores, x_ref, writers, readers, out_ref):
    length, heads = cum_cols.shape
    per_group = x_ref.shape[1] // channels
    tile = 128
    sc = lax.dot_general(
        readers, writers, (((1,), (1,)), ((), ())), preferred_element_type=F32
    )
    row = lax.broadcasted_iota(jnp.int32, (length, length), 0)
    col = lax.broadcasted_iota(jnp.int32, (length, length), 1)
    scores[...] = jnp.where(row >= col, sc, 0.0)

    base = pl.multiple_of(group * per_group, per_group)
    rows_all = cum_rows[pl.ds(base, per_group), :]
    cols_all = pltpu.roll(cum_cols[...], heads - base, axis=1)
    starts = list(range(0, length, tile))

    def weights(head, top, bottom):
        column = cols_all[top:bottom, head : head + 1]
        parts = []
        for left in range(0, bottom, tile):
            right = min(left + tile, bottom)
            gap = column - rows_all[head : head + 1, left:right]
            if right > top:
                gap = jnp.minimum(gap, 0.0)
            parts.append((jnp.exp2(gap) * scores[top:bottom, left:right]).astype(BF16))
        return parts[0] if len(parts) == 1 else jnp.concatenate(parts, axis=1)

    lane = lax.broadcasted_iota(jnp.int32, (1, 2 * channels), 1)
    for pair in range(per_group // 2):
        x_pair = x_ref[:, pair * 2 * channels : (pair + 1) * 2 * channels]
        for top in starts:
            bottom = min(top + tile, length)
            both = jnp.concatenate(
                [weights(2 * pair, top, bottom), weights(2 * pair + 1, top, bottom)], axis=0
            )
            mixed = jnp.dot(both, x_pair[:bottom], preferred_element_type=F32)
            out_ref[top:bottom, pair * 2 * channels : (pair + 1) * 2 * channels] = jnp.where(
                lane < channels, mixed[: bottom - top], mixed[bottom - top :]
            )


def diagonals(side, cumulative, inputs, write_vectors, read_vectors):
    length, heads = cumulative.shape
    width = inputs.shape[1]
    padded = -(-length // 128) * 128
    return pl.pallas_call(
        lambda *refs: diagonal_kernel(width // heads, *refs),
        in_specs=[SCALAR] + [WHOLE] * 4,
        out_specs=WHOLE,
        out_shape=jax.ShapeDtypeStruct((length, width // 2), F32),
        scratch_shapes=[
            pltpu.VMEM((heads, padded), F32),
            pltpu.VMEM((length, heads), F32),
            pltpu.VMEM((length, length), F32),
        ],
        compiler_params=pltpu.CompilerParams(vmem_limit_bytes=VMEM_LIMIT),
        cost_estimate=pl.CostEstimate(
            flops=length * length * width,
            bytes_accessed=3 * length * width,
            transcendentals=length * length * heads // 2,
        ),
    )(side, cumulative, inputs, write_vectors, read_vectors)


def scan_kernel(parts, side_ref, term_ref, out_hbm, out_ref, sems):
    along, chip_rows, rows, lanes = out_ref.shape
    rows = rows // 2

    def some(i, states):
        for k in range(along):
            logs = term_ref[k, i, 2 * rows // THIN].astype(F32)
            after = []
            for side in range(2):
                span = slice(side * rows, (side + 1) * rows)
                out_ref[k, i, span] = states[side].astype(BF16)
                decay = jnp.exp(logs[2 * side : 2 * side + 1] + logs[2 * side + 1 : 2 * side + 2])
                first = side * (rows // THIN)
                term = [term_ref[k, i, first + r].astype(F32) for r in range(rows // THIN)]
                after.append(decay * states[side] + jnp.concatenate(term, axis=0))
            states = tuple(after)
        return states

    states = (jnp.zeros((rows, lanes), F32),) * 2
    size = chip_rows // parts
    for part in range(parts):
        states = lax.fori_loop(part * size, (part + 1) * size, some, states)
        part_copy(parts, part, out_ref, out_hbm, sems).start()
    for part in range(parts):
        part_copy(parts, part, out_ref, out_hbm, sems).wait()


def entries(side, terms):
    along, chip_rows, thins, _, lanes = terms.shape
    return off_chip(scan_kernel, (along, chip_rows, (thins - 1) * THIN, lanes), side, terms)


def read_kernel(channels, mine, side_ref, cum_ref, c_ref, diagonal_ref, held_ref, *rest):
    if mine:
        late_diagonal, late_came = diagonal_ref, rest[0]
        rest, (diagonal_ref, came_ref, diagonal_sems, came_sems) = rest[:-4], rest[-4:]
    out_hbm, grown_ref, pick_ref, out_ref, sems = rest[-5:]
    half, _, columns = out_ref.shape
    bring = []
    for turn in range(half if mine else 0):
        size = came_ref.shape[1] // half
        part = pl.ds(turn * size, size)
        pair = (
            pltpu.make_async_copy(late_came.at[:, part], came_ref.at[:, part], came_sems.at[turn]),
            pltpu.make_async_copy(
                group_columns(late_diagonal, turn, columns),
                group_columns(diagonal_ref, turn, columns),
                diagonal_sems.at[turn],
            ),
        )
        for copy in pair:
            copy.start()
        bring.append(pair)
    state_size = c_ref.shape[1] // G
    grown_ref[...] = jnp.exp(cum_ref[...])
    pick_ref[...] = head_columns(columns, channels, cum_ref.shape[1])
    blocks_n, blocks_c, rows, lanes = held_ref.shape
    rows = rows // 2
    count = blocks_c // half
    copies = []
    for turn in range(half):
        group = side_ref[0] * half + turn
        decay = spread_heads(grown_ref[...], pick_ref[...], group * (columns // channels))
        readers = group_columns(c_ref, group, state_size)[...]
        if mine:
            readers = jnp.concatenate([readers, readers], axis=1)
        for copy in bring[turn] if mine else ():
            copy.wait()
        for j in range(count):
            sides = []
            for k in range(2):
                at = turn * count + j
                span = slice(k * rows, (k + 1) * rows)
                held = jnp.concatenate([held_ref[i, at, span] for i in range(blocks_n)], axis=0)
                if mine:
                    second = side_ref[0] == 1
                    came = jnp.concatenate([came_ref[i, at, span] for i in range(blocks_n)], axis=0)
                    logs = log_decays(came_ref[0, at, 2 * rows :])[k]
                    scale = jnp.exp(jnp.where(second, logs, 0.0))
                    start = scale * held.astype(F32) + jnp.where(second, came.astype(F32), 0.0)
                    held = jnp.concatenate(split_two(start), axis=0)
                sides.append(held)
            read = jnp.dot(readers, jnp.concatenate(sides, axis=1), preferred_element_type=F32)
            span = slice(2 * j * lanes, (2 * j + 2) * lanes)
            wide = slice(turn * columns + 2 * j * lanes, turn * columns + (2 * j + 2) * lanes)
            out_ref[turn, :, span] = (diagonal_ref[:, wide] + read * decay[:, span]).astype(BF16)
        copy = pltpu.make_async_copy(out_ref.at[turn], group_columns(out_hbm, group, columns), sems.at[turn])
        copy.start()
        copies.append(copy)
    for copy in copies:
        copy.wait()


def outputs(side, cumulative, read_vectors, diagonal, held, came=None, done=None):
    length, heads = cumulative.shape
    half = G // 2
    width = diagonal.shape[1] * 2
    columns = width // G
    in_specs = [SCALAR] + [WHOLE] * 4
    args = [side, cumulative, read_vectors, diagonal, held]
    aliases = {}
    extra = []
    if came is not None:
        in_specs[3] = LEFT
        args[3] = pltpu.with_memory_space_constraint(diagonal, pltpu.HBM)
        in_specs.append(LEFT)
        args.append(pltpu.with_memory_space_constraint(came, pltpu.HBM))
        extra = [
            pltpu.VMEM(diagonal.shape, F32),
            pltpu.VMEM(came.shape, BF16),
            pltpu.SemaphoreType.DMA((half,)),
            pltpu.SemaphoreType.DMA((half,)),
        ]
    if done is not None:
        in_specs.append(LEFT)
        aliases = {len(args): 0}
        args.append(done)
    return pl.pallas_call(
        lambda *refs: read_kernel(width // heads, came is not None, *refs),
        in_specs=in_specs,
        out_specs=LEFT,
        scratch_shapes=[
            pltpu.VMEM((length, heads), F32),
            pltpu.VMEM((2 * heads, columns), BF16),
            pltpu.VMEM((half, length, columns), BF16),
            pltpu.SemaphoreType.DMA((half,)),
        ] + extra,
        out_shape=jax.ShapeDtypeStruct((length, width), BF16),
        input_output_aliases=aliases,
        compiler_params=pltpu.CompilerParams(vmem_limit_bytes=VMEM_LIMIT),
        cost_estimate=pl.CostEstimate(
            flops=2 * length * 128 * width,
            bytes_accessed=2 * length * width,
            transcendentals=0,
        ),
    )(*args)


def shards(inputs, log_decay, write_vectors, read_vectors):
    chips = lax.axis_size("seq") * lax.axis_size("z")
    pieces_n = lax.axis_size("z")
    pieces_c = lax.axis_size("seq")
    own_side = lax.axis_index("c").astype(jnp.int32).reshape(1)
    other_side = 1 - own_side
    swap = [(0, 1), (1, 0)]

    cumulative, gone, inputs, write_vectors = first_states(
        other_side, log_decay, inputs, write_vectors, pieces_n, pieces_c
    )
    came = lax.ppermute(gone, "c", swap)
    kept = second_states(own_side, cumulative, inputs, write_vectors, pieces_n, pieces_c)
    term = joined(own_side, kept, came)

    terms = lax.all_to_all(term.reshape((chips,) + term.shape[2:]), ("z", "seq"), 0, 0, tiled=True)
    diagonal_own = diagonals(own_side, cumulative, inputs, write_vectors, read_vectors)
    terms, diagonal_own = lax.optimization_barrier((terms, diagonal_own))

    held = entries(own_side, terms.reshape(term.shape))
    held = lax.all_to_all(held.reshape((chips,) + held.shape[2:]), ("z", "seq"), 0, 0, tiled=True)
    diagonal_other = diagonals(other_side, cumulative, inputs, write_vectors, read_vectors)
    held, diagonal_other = lax.optimization_barrier((held, diagonal_other))
    held = held.reshape(term.shape[:2] + held.shape[1:])

    held_other = lax.ppermute(given(own_side, held, kept), "c", swap)
    done = outputs(own_side, cumulative, read_vectors, diagonal_own, held, came=came)
    return outputs(other_side, cumulative, read_vectors, diagonal_other, held_other, done=done)


def solution(mesh):
    seq, head = mesh.devices.shape
    fine = Mesh(mesh.devices.reshape(seq, head // 2, 2), ("seq", "z", "c"))
    spec = P(("seq", "z", "c"), None)
    return jax.shard_map(
        shards, mesh=fine, in_specs=(spec,) * 4, out_specs=spec, check_vma=False
    )
```
